32 devices in a mesh: dp: 2 (over x), mx: 4 (over z), my: 4 (over y, core).
Axes of the slice: x: 2, y: 2, z: 4, core: 2. Of those that a mesh axis runs over, the one named last changes fastest.
Arguments:
- inputs: bfloat16 [2048, 6144], P(('dp', 'my'), 'mx'), may hold values from -6 to 6
- hidden_in: bfloat16 [2048, 24576], P(('dp', 'mx'), 'my'), may hold values from -6 to 6
- out_grad: bfloat16 [2048, 6144], P(('dp', 'my'), 'mx'), may hold values from -6 to 6
- up_weight: bfloat16 [6144, 24576], P('mx', 'my'), may hold values from -0.078125 to 0.078125
- down_weight: bfloat16 [24576, 6144], P('my', 'mx'), may hold values from -0.0390625 to 0.0390625
Outputs:
- inputs_grad: bfloat16 [2048, 6144], P(('dp', 'my'), 'mx')
- up_grad: bfloat16 [6144, 24576], P('mx', 'my')
- down_grad: bfloat16 [24576, 6144], P('my', 'mx')
The draws below stay inside these ranges and needn't reach their ends.
All inputs are finite; a program needn't handle non-finite values.
Results may differ from the reference program's by a relative error of at most 0.0059.
Values may be sent and summed in bfloat16 or wider, within the bound.
A program may use at most 192 MiB of HBM per device.

```python
import jax
import jax.numpy as jnp
from jax import lax

D = 6144
FF = 24576
TOK_DEV = 1024
TOKENS = 2048
N_DP = 2


def shard_levels(key, shape, split, low, top_value):
    loudness, own = 1.0, jax.random.fold_in(key, 6)
    for dim, blocks in split:
        draws = jnp.exp(jax.random.uniform(jax.random.fold_in(own, dim), (blocks,), jnp.float32, low / len(split), top_value / len(split)))
        loudness = loudness * jnp.repeat(draws, shape[dim] // blocks).reshape([-1 if axis == dim else 1 for axis in range(len(shape))])
    return loudness


def gaussian(stream_key, dims, spread, reach, pieces=(), kind=jnp.bfloat16):
    entries = jax.random.normal(stream_key, dims, jnp.float32) * spread
    if len(pieces) > 0:
        entries = shard_levels(stream_key, dims, pieces, -0.22, 0.18) * entries
    return jnp.clip(entries, min=-reach, max=reach).astype(kind)


def setup_inputs(seed: int = 0) -> dict:
    key_of = jax.random.split(jax.random.key(seed), 6)
    inputs = gaussian(key_of[0], (TOKENS, D), 1.0, 6.0, ((0, 8), (1, 4)))
    hidden_in = gaussian(key_of[1], (TOKENS, FF), 1.5, 6.0, ((0, 8), (1, 4)))
    out_grad = gaussian(key_of[2], (TOKENS, D), 1.0, 6.0, ((0, 8), (1, 4)))
    up_weight = gaussian(key_of[3], (D, FF), D ** -0.5, 0.078125, ((0, 4), (1, 4)))
    down_weight = gaussian(key_of[4], (FF, D), FF ** -0.5, 0.0390625, ((0, 4), (1, 4)))
    return dict(inputs=inputs, hidden_in=hidden_in, out_grad=out_grad, up_weight=up_weight, down_weight=down_weight)


def gelu_value(value):
    return 0.5 * value * (1.0 + lax.erf(value * 0.7071067811865476))

def gelu_slope(value):
    return 0.5 * (1.0 + lax.erf(value * 0.7071067811865476)) + value * jnp.exp(-0.5 * value * value) * 0.3989422804014327

def reference(inputs, hidden_in, out_grad, up_weight, down_weight):
    pre_value = hidden_in.astype(jnp.float32)
    act = gelu_value(pre_value).astype(jnp.bfloat16)
    act_grad = jnp.dot(out_grad, down_weight.T, preferred_element_type=jnp.float32)
    pre_grad = (act_grad * gelu_slope(pre_value)).astype(jnp.bfloat16)
    inputs_grad = jnp.dot(pre_grad, up_weight.T, preferred_element_type=jnp.float32).astype(jnp.bfloat16)
    grad_scale = 1.0 / jnp.sqrt(jnp.float32(TOKENS))
    down_total = jnp.zeros((FF, D), jnp.float32)
    up_total = jnp.zeros((D, FF), jnp.float32)
    for half in range(N_DP):
        first_row = half * TOK_DEV
        act_block = act[first_row:first_row + TOK_DEV]
        grad_block = out_grad[first_row:first_row + TOK_DEV]
        input_block = inputs[first_row:first_row + TOK_DEV]
        pre_block = pre_grad[first_row:first_row + TOK_DEV]
        down_part = (jnp.dot(act_block.T, grad_block, preferred_element_type=jnp.float32) * grad_scale).astype(jnp.bfloat16)
        up_part = (jnp.dot(input_block.T, pre_block, preferred_element_type=jnp.float32) * grad_scale).astype(jnp.bfloat16)
        down_part = lax.optimization_barrier(down_part)
        up_part = lax.optimization_barrier(up_part)
        down_total = down_total + down_part.astype(jnp.float32)
        up_total = up_total + up_part.astype(jnp.float32)
    return (inputs_grad, up_total.astype(jnp.bfloat16), down_total.astype(jnp.bfloat16))
```

```python
import jax
import jax.numpy as jnp
from jax import lax
from jax.sharding import PartitionSpec as P

BF16, F32 = jnp.bfloat16, jnp.float32


def gelu_value(value):
    return 0.5 * value * (1.0 + lax.erf(value * 0.7071067811865476))


def gelu_slope(value):
    return (
        0.5 * (1.0 + lax.erf(value * 0.7071067811865476))
        + value * jnp.exp(-0.5 * value * value) * 0.3989422804014327
    )


def swap(block):
    return lax.ppermute(block, "dp", [(0, 1), (1, 0)])


def add(first, *others):
    total = first.astype(F32)
    for other in others:
        total = total + other.astype(F32)
    return total


def after(value, *earlier):
    for other in earlier:
        corner = other[(0,) * (other.ndim - 2)][:16, :128].astype(F32)
        value = value + jnp.minimum(jnp.max(jnp.abs(corner)), 0.0)
    return value


def line_gather(block):
    n, p = lax.axis_size("mx"), lax.axis_index("mx")
    up, down = [block], [block]
    for s in range(1, n):
        up.append(lax.ppermute(up[-1], "mx", [(i, i + 1) for i in range(s - 1, n - 1)]))
        down.append(lax.ppermute(down[-1], "mx", [(i, i - 1) for i in range(1, n - s + 1)]))
    slots = [block] + [jnp.where(p >= r, up[r], down[n - r]) for r in range(1, n)]
    return jnp.concatenate(slots, axis=0), (up[-2], down[-2])


def line_scatter(part):
    n = part.shape[0]
    up = down = None
    seen = []
    for s in range(1, n):
        send_up = part[s] if up is None else add(part[s], up).astype(BF16)
        send_down = part[n - s] if down is None else add(part[n - s], down).astype(BF16)
        up = lax.ppermute(send_up, "mx", [(i, i + 1) for i in range(s)])
        down = lax.ppermute(send_down, "mx", [(i, i - 1) for i in range(n - s, n)])
        seen.append((up, down))
    return add(part[0], up, down), seen[-2]


def rows_in_line_order(block):
    n, p = lax.axis_size("mx"), lax.axis_index("mx")
    both = jnp.stack([block, swap(block)])
    whole = lax.all_gather(both, "my", axis=1, tiled=True)
    whole = whole.reshape(2, n, whole.shape[1] // n, whole.shape[2])
    slots = [lax.dynamic_index_in_dim(whole, (p - r) % n, 1, False) for r in range(n)]
    return jnp.concatenate(slots, axis=0).reshape(-1, block.shape[1])


def scatter_rows(part):
    me = lax.axis_index("my")
    bit = 1
    while part.shape[1] > 1:
        pairs = part.reshape(2, part.shape[1] // 2, 2, *part.shape[2:])
        mine = (me // bit) % 2
        keep = jnp.where(mine == 0, pairs[:, :, 0], pairs[:, :, 1])
        send = jnp.where(mine == 0, pairs[:, :, 1], pairs[:, :, 0]).astype(BF16)
        got = lax.ppermute(send, "my", [(i, i ^ bit) for i in range(lax.axis_size("my"))])
        part = add(keep, got)
        bit *= 2
    return add(part[0, 0], swap(part[1, 0].astype(BF16))).astype(BF16)


def per_device(inputs, hidden_in, out_grad, up_weight, down_weight):
    n, p, dp = lax.axis_size("mx"), lax.axis_index("mx"), lax.axis_index("dp")
    n_my = lax.axis_size("my")
    total_tokens = out_grad.shape[0] * n_my * lax.axis_size("dp")
    grad_scale = 1.0 / jnp.sqrt(jnp.float32(total_tokens))
    rows, ff = hidden_in.shape
    width = inputs.shape[1]
    half = ff // 2
    chunks = 4
    w = half // chunks

    grad_rows = rows_in_line_order(out_grad)

    hidden = []
    for c in range(chunks):
        low, high = hidden_in[:, c * w:(c + 1) * w], hidden_in[:, half + c * w:half + (c + 1) * w]
        mine, other = jnp.where(dp == 0, low, high), jnp.where(dp == 0, high, low)
        hidden.append(jnp.concatenate([mine, swap(other)], axis=0).astype(F32))

    input_rows = rows_in_line_order(after(inputs.astype(F32), grad_rows).astype(BF16))

    down_grad = jnp.zeros(down_weight.shape, BF16)
    up_grad = jnp.zeros(up_weight.shape, BF16)
    inputs_part = None
    act_all, act_mid, down_own, down_got, up_own, up_got = [], [], [], [], [], []
    part_mid = ()

    def gather_act(c):
        gates = act_mid[c - 1] if c > 0 else ()
        act = after(gelu_value(hidden[c]), *gates).astype(BF16)
        whole, middle = line_gather(act)
        act_all.append(whole)
        act_mid.append(middle)

    gather_act(0)
    for c in range(chunks):
        own = (
            jnp.einsum("tf,td->fd", act_all[c], grad_rows, preferred_element_type=F32) * grad_scale
        ).astype(BF16)
        got = swap(own)
        down_own.append(own)
        down_got.append(got)
        down_grad = lax.dynamic_update_slice(down_grad, jnp.where(dp == 0, own, got), (c * w, 0))
        down_grad = lax.dynamic_update_slice(
            down_grad, jnp.where(dp == 0, got, own), (half + c * w, 0)
        )

        weight = lax.dynamic_slice_in_dim(down_weight, dp * half + c * w, w, 0)
        part = jnp.einsum("td,fd->tf", grad_rows, weight, preferred_element_type=F32)
        gates = part_mid
        if c == 0:
            gates += act_mid[0]
        if c > 0:
            gates += (down_own[c - 1],)
        if c > 1:
            gates += (down_got[c - 2],)
        part = after(part, *gates).astype(BF16).reshape(n, 2 * rows, w)
        act_grad, part_mid = line_scatter(part)
        gates = ()
        if c + 1 < chunks:
            gather_act(c + 1)
            gates += act_mid[c + 1]
        else:
            gates += (down_got[c],)
        if c > 1:
            gates += (up_got[c - 2],)
        pre_grad = after(act_grad * gelu_slope(hidden[c]), *gates).astype(BF16)
        pre_all, _ = line_gather(pre_grad)

        own = jnp.einsum("td,tf->df", input_rows, pre_all, preferred_element_type=F32) * grad_scale
        if c == chunks - 1:
            own = after(own, up_got[c - 1])
        own = own.astype(BF16)
        got = swap(own)
        up_own.append(own)
        up_got.append(got)
        up_grad = lax.dynamic_update_slice(up_grad, jnp.where(dp == 0, own, got), (0, c * w))
        up_grad = lax.dynamic_update_slice(
            up_grad, jnp.where(dp == 0, got, own), (0, half + c * w)
        )

        weight = lax.dynamic_slice_in_dim(up_weight, dp * half + c * w, w, 1)
        term = jnp.einsum("tf,df->td", pre_all, weight, preferred_element_type=F32)
        inputs_part = term if inputs_part is None else inputs_part + term
    inputs_part = after(inputs_part, up_own[-1])

    slots = inputs_part.reshape(n, 2, rows, width)
    blocks = [lax.dynamic_index_in_dim(slots, (p - q) % n, 0, False) for q in range(n)]
    part = jnp.concatenate(blocks, axis=1)
    inputs_grad = scatter_rows(part.reshape(2, n_my, -1, width))
    return inputs_grad, up_grad, down_grad


def solution(mesh):
    return jax.shard_map(
        per_device,
        mesh=mesh,
        in_specs=(
            P(("dp", "my"), "mx"),
            P(("dp", "mx"), "my"),
            P(("dp", "my"), "mx"),
            P("mx", "my"),
            P("my", "mx"),
        ),
        out_specs=(P(("dp", "my"), "mx"), P("mx", "my"), P("my", "mx")),
        check_vma=False,
    )
```
